32 devices in a mesh: gx: 4 (over y, core), pa: 8 (over z, x).
Axes of the slice: x: 2, y: 2, z: 4, core: 2. Of those that a mesh axis runs over, the one named last changes fastest.
Arguments:
- u_factor: float32 [64, 32768], P(None, 'gx'), may hold values from -160 to 160, as said below
- v_factor: float32 [64, 65536], P(None, 'pa'), may hold values from -160 to 160, as said below
- mass_table: float32 [4, 16], replicated, may hold values from -2 to 2
- diffusivity_table: float32 [4, 16], replicated, may hold values from 0.2 to 1
- material_index: int32 [4, 32768], P(None, 'gx'), may hold values from 0 to 15
- band_weights: float32 [4, 3, 65536], P(None, None, 'pa'), may hold values from -5 to 5
- band_offsets: int32 [4, 3], replicated, may hold values from -4 to 4, as said below
- core_matrix: float32 [64, 64], replicated, may hold values from -4 to 4
- sketch_seed: int32 [1], replicated, may hold values from 0 to 65520
Outputs:
- u_next: float32 [64, 32768], P(None, 'gx')
- v_next: float32 [64, 65536], P(None, 'pa')
- core_next: float32 [64, 64], replicated
The draws below stay inside these ranges and needn't reach their ends.
Inputs may be any that keep to these rules, and one draw needn't show every extreme that they name: `u_factor`: each factor is finite and its rows are of mixed scales. `v_factor`: each factor is finite and its rows are of mixed scales. `band_offsets`: some tap reaches each end of the band.
All inputs are finite; a program needn't handle non-finite values.
Results may differ from the reference program's by a relative error of at most 0.0003.
Values sent between devices are 32-bit elements; how exact they have to be, the bound alone decides.
A program may use at most 128 MiB of HBM per device.

```python
import math
import jax
import jax.numpy as jnp
from jax import lax

RANK = 64
STENCILS = 4
MATERIALS = 16
TAPS = 3
BAND = 4
WIDE = 256
NX = 32768
NP = 65536


def factor_draw(key, rows):
    keys = jax.random.split(key, 3)
    position = jnp.arange(rows, dtype=jnp.float32) / (rows - 1)
    rise = (1.0 + 2.0 * position)[None, :]
    column_scale = jnp.exp(jax.random.uniform(keys[2], (RANK, 1), jnp.float32, math.log(0.3), math.log(3.0)))
    base = jnp.clip(jax.random.normal(keys[0], (RANK, rows), jnp.float32), -4.0, 4.0)
    row_scale = jnp.exp(jax.random.uniform(keys[1], (1, rows), jnp.float32, 0.0, math.log(10.0)))
    return base * rise * row_scale * column_scale / 4.0


def draw_u_factor(key, part):
    return factor_draw(jax.random.fold_in(key, 101), NX)


def draw_v_factor(key, part):
    return factor_draw(jax.random.fold_in(key, 202), NP)


def draw_band_offsets(key, part):
    keys = jax.random.split(jax.random.fold_in(key, 303), 2)
    offsets = jax.random.randint(keys[0], (STENCILS, TAPS), -BAND, BAND + 1)
    picks = jax.random.randint(keys[1], (2,), 0, STENCILS)
    offsets = offsets.at[picks[0], 0].set(-BAND)
    offsets = offsets.at[picks[1], 1].set(BAND)
    return offsets.astype(jnp.int32)


def draw_core_matrix(key, part):
    keys = jax.random.split(jax.random.fold_in(key, 404), 2)
    diagonal = jax.random.uniform(keys[0], (RANK,), jnp.float32, 2.0, 4.0)
    spread = jnp.clip(0.1 * jax.random.normal(keys[1], (RANK, RANK), jnp.float32), -0.5, 0.5)
    eye = jnp.eye(RANK, dtype=jnp.float32)
    return eye * diagonal[:, None] + (1.0 - eye) * spread


def place_ends(entries, key, low, top_value):
    extent = entries.shape
    spot = [jax.random.randint(jax.random.fold_in(key, axis), (), 0, extent[axis]) for axis in range(len(extent))]
    entries = entries.at[tuple(spot)].set(low)
    longest = extent.index(max(extent))
    spot[longest] = (spot[longest] + 1) % extent[longest]
    return entries.at[tuple(spot)].set(top_value)


def levels(own_key, dims, shards, smallest, high):
    level = 1.0
    for axis_at, parts in shards:
        heights = jax.random.uniform(jax.random.fold_in(jax.random.fold_in(own_key, 6), axis_at), (parts,), jnp.float32, smallest / len(shards), high / len(shards))
        level = level * jnp.repeat(jnp.exp(heights), dims[axis_at] // parts).reshape((-1,) + (1,) * (len(dims) - 1 - axis_at))
    return level


def noise(rng, shape, deviation, reach, cuts=(), kind=jnp.bfloat16):
    entries = jax.random.normal(rng, shape, jnp.float32) * deviation
    if len(cuts) > 0:
        entries = levels(rng, shape, cuts, -0.22, 0.18) * entries
    return jnp.clip(entries, min=-reach, max=reach).astype(kind)


def setup_inputs(seed: int = 0) -> dict:
    streams_of = jax.random.split(jax.random.key(seed), 10)
    return {
        "u_factor": draw_u_factor(jax.random.fold_in(streams_of[9], 71), 0),
        "v_factor": draw_v_factor(jax.random.fold_in(streams_of[9], 71), 0),
        "mass_table": jnp.clip(jax.random.uniform(streams_of[2], (STENCILS, MATERIALS), jnp.float32, -2.0, 2.0), -2.0, 2.0),
        "diffusivity_table": jnp.clip(jnp.exp(jax.random.uniform(streams_of[3], (STENCILS, MATERIALS), jnp.float32, math.log(0.2), math.log(1.0))), 0.2, 1.0),
        "material_index": place_ends(jax.random.randint(streams_of[4], (STENCILS, NX), 0, MATERIALS), jax.random.fold_in(streams_of[4], 1), 0, MATERIALS - 1).astype(jnp.int32),
        "band_weights": noise(streams_of[5], (STENCILS, TAPS, NP), 1.0, 5.0, ((2, 8),), jnp.float32),
        "band_offsets": draw_band_offsets(jax.random.fold_in(streams_of[9], 71), 0),
        "core_matrix": draw_core_matrix(jax.random.fold_in(streams_of[9], 71), 0),
        "sketch_seed": jax.random.randint(streams_of[8], (1,), 0, 65521).astype(jnp.int32),
    }


def make_sketch(sketch_seed):
    rows_idx = lax.broadcasted_iota(jnp.int32, (WIDE, RANK), 0)
    cols_idx = lax.broadcasted_iota(jnp.int32, (WIDE, RANK), 1)
    first = (rows_idx * 131 + cols_idx * 977 + sketch_seed[0]) % 65521
    second = first * 7919 % 65521
    upper = second // 256
    lower = second % 256
    third = (upper * upper * 15 + 512 * upper * lower + lower * lower) % 65521
    fourth = (third * 30011 + rows_idx * 17 + cols_idx) % 65521
    return ((fourth.astype(jnp.float32) + 0.5) / 65521.0 - 0.5) * 3.4641

def matmul(left_m, right_m):
    return jnp.dot(left_m.astype(jnp.float32), right_m.astype(jnp.float32), precision=lax.Precision.HIGHEST, preferred_element_type=jnp.float32)

def solve_lower(lower_m, rhs, transpose):
    return lax.linalg.triangular_solve(lower_m, rhs, left_side=True, lower=True, transpose_a=transpose)

def widen_space(u_factor, mass_table, diffusivity_table, material_index):
    choices_m = jnp.arange(MATERIALS, dtype=jnp.int32)
    onehot = (material_index[:, None, :] == choices_m[None, :, None]).astype(jnp.float32)
    mass_cell = jnp.sum(mass_table[:, :, None] * onehot, axis=1)
    diffusion = jnp.sum(diffusivity_table[:, :, None] * onehot, axis=1)
    padded = jnp.pad(u_factor, ((0, 0), (1, 1)))
    laplace = padded[:, 2:] - 2.0 * u_factor + padded[:, :-2]
    blocks = mass_cell[:, None, :] * u_factor[None] + diffusion[:, None, :] * laplace[None]
    return blocks.reshape(STENCILS * RANK, u_factor.shape[1])

def widen_param(v_factor, band_weights, band_offsets):
    count = v_factor.shape[1]
    padded = jnp.pad(v_factor, ((0, 0), (BAND, BAND)))
    blocks = []
    for stencil in range(STENCILS):
        total = jnp.zeros(v_factor.shape, jnp.float32)
        for tap_index in range(TAPS):
            start = (BAND + band_offsets[stencil, tap_index]).astype(jnp.int32)
            moved = lax.dynamic_slice_in_dim(padded, start, count, 1)
            total = total + band_weights[stencil, tap_index][None, :] * moved
        blocks.append(total)
    return jnp.concatenate(blocks, axis=0)

def truncate(lower_u, lower_v, core_matrix, sketch_seed):
    block_core = jnp.kron(jnp.eye(STENCILS, dtype=jnp.float32), core_matrix)
    core_wide = matmul(matmul(lower_u.T, block_core), lower_v)
    range_y = matmul(core_wide, make_sketch(sketch_seed))
    lower_y = jnp.linalg.cholesky(matmul(range_y.T, range_y))
    left = solve_lower(lower_y, range_y.T, False).T
    back_z = matmul(core_wide.T, left)
    core_next = jnp.linalg.cholesky(matmul(back_z.T, back_z))
    right = solve_lower(core_next, back_z.T, False).T
    map_u = solve_lower(lower_u, left, True)
    map_v = solve_lower(lower_v, right, True)
    return (map_u, map_v, core_next)

def reference(u_factor, v_factor, mass_table, diffusivity_table, material_index, band_weights, band_offsets, core_matrix, sketch_seed):
    space_wide = widen_space(u_factor, mass_table, diffusivity_table, material_index)
    param_wide = widen_param(v_factor, band_weights, band_offsets)
    gram_u = matmul(space_wide, space_wide.T) / NX
    gram_v = matmul(param_wide, param_wide.T) / NP
    lower_u = jnp.linalg.cholesky(gram_u)
    lower_v = jnp.linalg.cholesky(gram_v)
    map_u, map_v, core_next = truncate(lower_u, lower_v, core_matrix, sketch_seed)
    u_next = matmul(map_u.T, space_wide)
    v_next = matmul(map_v.T, param_wide)
    return (u_next, v_next, core_next)
```

```python
import jax
import jax.numpy as jnp
from jax import lax
from jax.sharding import PartitionSpec as P

BAND = 4


def extended(cells, sides, width):
    for axis, dim in sides:
        count = lax.axis_size(axis)
        ends = count - 1
        head = lax.slice_in_dim(cells, 0, width, axis=dim)
        tail = lax.slice_in_dim(cells, cells.shape[dim] - width, cells.shape[dim], axis=dim)
        cells = jnp.concatenate(
            [
                lax.ppermute(tail, axis, [(i, (i + 1) % count) for i in range(ends)]),
                cells,
                lax.ppermute(head, axis, [((i + 1) % count, i) for i in range(ends)]),
            ],
            axis=dim,
        )
    return cells


def make_sketch(sketch_seed, wide, rank):
    rows_idx = lax.broadcasted_iota(jnp.int32, (wide, rank), 0)
    cols_idx = lax.broadcasted_iota(jnp.int32, (wide, rank), 1)
    first = (rows_idx * 131 + cols_idx * 977 + sketch_seed[0]) % 65521
    second = first * 7919 % 65521
    upper = second // 256
    lower = second % 256
    third = (upper * upper * 15 + 512 * upper * lower + lower * lower) % 65521
    fourth = (third * 30011 + rows_idx * 17 + cols_idx) % 65521
    return ((fourth.astype(jnp.float32) + 0.5) / 65521.0 - 0.5) * 3.4641


def matmul(left_m, right_m):
    return jnp.dot(
        left_m, right_m, precision=lax.Precision.HIGHEST, preferred_element_type=jnp.float32
    )


def solve_lower(lower_m, rhs, transpose):
    return lax.linalg.triangular_solve(
        lower_m, rhs, left_side=True, lower=True, transpose_a=transpose
    )


def gram_of(wide_rows):
    return lax.dot_general(
        wide_rows,
        wide_rows,
        (((1,), (1,)), ((), ())),
        precision=lax.Precision.HIGHEST,
        preferred_element_type=jnp.float32,
    )


def widen_space(u_factor, mass_table, diffusivity_table, material_index):
    stencils = mass_table.shape[0]
    choices_m = jnp.arange(mass_table.shape[1], dtype=jnp.int32)
    onehot = (material_index[:, None, :] == choices_m[None, :, None]).astype(jnp.float32)
    mass_cell = jnp.sum(mass_table[:, :, None] * onehot, axis=1)
    diffusion = jnp.sum(diffusivity_table[:, :, None] * onehot, axis=1)
    padded = extended(u_factor, (("gx", 1),), 1)
    laplace = padded[:, 2:] - 2.0 * u_factor + padded[:, :-2]
    blocks = mass_cell[:, None, :] * u_factor[None] + diffusion[:, None, :] * laplace[None]
    return blocks.reshape(stencils * u_factor.shape[0], u_factor.shape[1])


def widen_param(v_factor, band_weights, band_offsets):
    count = v_factor.shape[1]
    padded = extended(v_factor, (("pa", 1),), BAND)
    blocks = []
    for stencil in range(band_weights.shape[0]):
        total = jnp.zeros(v_factor.shape, jnp.float32)
        for tap_index in range(band_weights.shape[1]):
            start = BAND + band_offsets[stencil, tap_index]
            moved = lax.dynamic_slice_in_dim(padded, start, count, 1)
            total = total + band_weights[stencil, tap_index][None, :] * moved
        blocks.append(total)
    return jnp.concatenate(blocks, axis=0)


def truncate(gram_u, gram_v, core_matrix, sketch_seed):
    rank = core_matrix.shape[0]
    wide = gram_v.shape[0]
    lower_v = jnp.linalg.cholesky(gram_v)
    mixed = matmul(lower_v, make_sketch(sketch_seed, wide, rank))
    blocks = mixed.reshape(wide // rank, rank, rank)
    base_u = jnp.concatenate([matmul(core_matrix, b) for b in blocks], axis=0)
    seen_u = matmul(gram_u, base_u)
    lower_y = jnp.linalg.cholesky(matmul(base_u.T, seen_u))
    both = solve_lower(lower_y, jnp.concatenate([base_u.T, seen_u.T], axis=1), False)
    map_u_t = both[:, :wide]
    back_t = jnp.concatenate(
        [
            matmul(both[:, wide + k * rank : wide + (k + 1) * rank], core_matrix)
            for k in range(wide // rank)
        ],
        axis=1,
    )
    core_next = jnp.linalg.cholesky(matmul(matmul(back_t, gram_v), back_t.T))
    map_v_t = solve_lower(core_next, back_t, False)
    return (map_u_t, map_v_t, core_next)


def local(
    u_factor,
    v_factor,
    mass_table,
    diffusivity_table,
    material_index,
    band_weights,
    band_offsets,
    core_matrix,
    sketch_seed,
):
    space_wide = widen_space(u_factor, mass_table, diffusivity_table, material_index)
    param_wide = widen_param(v_factor, band_weights, band_offsets)
    cells_total = u_factor.shape[1] * lax.axis_size("gx")
    samples_total = v_factor.shape[1] * lax.axis_size("pa")
    gram_u = lax.psum(gram_of(space_wide), "gx")
    gram_v = lax.psum(gram_of(param_wide), "pa")
    map_u_t, map_v_t, core_next = truncate(
        gram_u / cells_total, gram_v / samples_total, core_matrix, sketch_seed
    )
    u_next = matmul(map_u_t, space_wide)
    v_next = matmul(map_v_t, param_wide)
    return (u_next, v_next, core_next)


def solution(mesh):
    return jax.shard_map(
        local,
        mesh=mesh,
        in_specs=(
            P(None, "gx"),
            P(None, "pa"),
            P(),
            P(),
            P(None, "gx"),
            P(None, None, "pa"),
            P(),
            P(),
            P(),
        ),
        out_specs=(P(None, "gx"), P(None, "pa"), P()),
        check_vma=False,
    )
```

```python
import functools

import jax
import jax.numpy as jnp
from jax import lax
from jax.experimental import pallas as pl
from jax.experimental.pallas import tpu as pltpu
from jax.sharding import PartitionSpec as P

BAND = 4


def extended(cells, sides, width):
    for axis, dim in sides:
        count = lax.axis_size(axis)
        ends = count - 1
        head = lax.slice_in_dim(cells, 0, width, axis=dim)
        tail = lax.slice_in_dim(cells, cells.shape[dim] - width, cells.shape[dim], axis=dim)
        cells = jnp.concatenate(
            [
                lax.ppermute(tail, axis, [(i, (i + 1) % count) for i in range(ends)]),
                cells,
                lax.ppermute(head, axis, [((i + 1) % count, i) for i in range(ends)]),
            ],
            axis=dim,
        )
    return cells


def make_sketch(sketch_seed, wide, rank):
    rows_idx = lax.broadcasted_iota(jnp.int32, (wide, rank), 0)
    cols_idx = lax.broadcasted_iota(jnp.int32, (wide, rank), 1)
    first = (rows_idx * 131 + cols_idx * 977 + sketch_seed[0]) % 65521
    second = first * 7919 % 65521
    upper = second // 256
    lower = second % 256
    third = (upper * upper * 15 + 512 * upper * lower + lower * lower) % 65521
    fourth = (third * 30011 + rows_idx * 17 + cols_idx) % 65521
    return ((fourth.astype(jnp.float32) + 0.5) / 65521.0 - 0.5) * 3.4641


def matmul(left_m, right_m):
    return jnp.dot(
        left_m, right_m, precision=lax.Precision.HIGHEST, preferred_element_type=jnp.float32
    )


def solve_lower(lower_m, rhs, transpose):
    return lax.linalg.triangular_solve(
        lower_m, rhs, left_side=True, lower=True, transpose_a=transpose
    )


def gram_of(wide_rows):
    return lax.dot_general(
        wide_rows,
        wide_rows,
        (((1,), (1,)), ((), ())),
        precision=lax.Precision.HIGHEST,
        preferred_element_type=jnp.float32,
    )


def widen_space(u_factor, mass_table, diffusivity_table, material_index):
    stencils = mass_table.shape[0]
    choices_m = jnp.arange(mass_table.shape[1], dtype=jnp.int32)
    onehot = (material_index[:, None, :] == choices_m[None, :, None]).astype(jnp.float32)
    mass_cell = jnp.sum(mass_table[:, :, None] * onehot, axis=1)
    diffusion = jnp.sum(diffusivity_table[:, :, None] * onehot, axis=1)
    padded = extended(u_factor, (("gx", 1),), 1)
    laplace = padded[:, 2:] - 2.0 * u_factor + padded[:, :-2]
    blocks = mass_cell[:, None, :] * u_factor[None] + diffusion[:, None, :] * laplace[None]
    return blocks.reshape(stencils * u_factor.shape[0], u_factor.shape[1])


def widen_param(v_factor, band_weights, band_offsets):
    count = v_factor.shape[1]
    padded = extended(v_factor, (("pa", 1),), BAND)
    blocks = []
    for stencil in range(band_weights.shape[0]):
        total = jnp.zeros(v_factor.shape, jnp.float32)
        for tap_index in range(band_weights.shape[1]):
            start = BAND + band_offsets[stencil, tap_index]
            moved = lax.dynamic_slice_in_dim(padded, start, count, 1)
            total = total + band_weights[stencil, tap_index][None, :] * moved
        blocks.append(total)
    return jnp.concatenate(blocks, axis=0)


def dot_nn(a, b):
    return lax.dot_general(a, b, (((1,), (0,)), ((), ())), precision=lax.Precision.HIGHEST, preferred_element_type=jnp.float32)


def dot_nt(a, b):
    return lax.dot_general(a, b, (((1,), (1,)), ((), ())), precision=lax.Precision.HIGHEST, preferred_element_type=jnp.float32)


def dot_tn(a, b):
    return lax.dot_general(a, b, (((0,), (0,)), ((), ())), precision=lax.Precision.HIGHEST, preferred_element_type=jnp.float32)


def eliminate(block, first):
    tile = 8
    count = block.shape[0] // tile
    lanes = 128
    wide = block.shape[1] // lanes
    rows = [block[tile * i : tile * (i + 1), :] for i in range(count)]
    sub = lax.broadcasted_iota(jnp.int32, (tile, lanes), 0)

    def spread(x):
        return jnp.concatenate([x] * wide, axis=1) if wide > 1 else x

    for q in range(count):
        at = first + tile * q
        cols = [
            {i: jnp.broadcast_to(rows[i][:, at + k : at + k + 1], (tile, lanes)) for i in range(q, count)}
            for k in range(tile)
        ]
        for j in range(tile):
            scale = lax.rsqrt(cols[j][q][j : j + 1, :])
            low = {i: cols[j][i] * scale for i in range(q, count)}
            for k in range(j + 1, tile):
                pivot = low[q][k : k + 1, :]
                for i in range(q, count):
                    cols[k][i] = cols[k][i] - low[i] * pivot
            own = rows[q][j : j + 1, :] * spread(scale)
            below = spread(jnp.where(sub > j, low[q], 0.0))
            rows[q] = jnp.where(spread(sub) == j, own, rows[q] - below * own)
            for i in range(q + 1, count):
                rows[i] = rows[i] - spread(low[i]) * own
    return jnp.concatenate(rows, axis=0)


def chain_kernel(rank, cells, samples, gram_u_ref, gram_v_ref, core_ref, sketch_ref, map_u_ref, map_v_ref, core_next_ref, gv, upper):
    wide = gram_u_ref.shape[0]
    gv[...] = gram_v_ref[...] * (1.0 / samples)
    for p in range(wide // rank):
        left = (p * rank) // 128 * 128
        low = p * rank
        part = gv[low : low + rank, left:]
        if p > 0:
            part = part - dot_tn(upper[:low, low : low + rank], upper[:low, left:])
        part = eliminate(part, low - left)
        row_at = lax.broadcasted_iota(jnp.int32, part.shape, 0) + low
        col_at = lax.broadcasted_iota(jnp.int32, part.shape, 1) + left
        upper[low : low + rank, left:] = jnp.where(col_at >= row_at, part, 0.0)
        if left > 0:
            upper[low : low + rank, :left] = jnp.zeros((rank, left), jnp.float32)
    core = core_ref[...]
    base = dot_nt(dot_nn(sketch_ref[...], upper[...]), core)
    seen = dot_nn(base, gram_u_ref[...] * (1.0 / cells))
    fill = jnp.zeros((128 - rank, wide), jnp.float32)
    square = dot_nt(base, jnp.concatenate([seen, fill], axis=0))
    back = dot_nn(seen, core)
    done = eliminate(jnp.concatenate([square, base, back], axis=1), 0)
    map_u_ref[...] = done[:, 128 : 128 + wide]
    back = done[:, 128 + wide :]
    square = dot_nt(dot_nn(back, gv[...]), jnp.concatenate([back, fill], axis=0))
    done = eliminate(jnp.concatenate([square, back], axis=1), 0)
    map_v_ref[...] = done[:, 128:]
    factor = done[:, :128]
    row_at = lax.broadcasted_iota(jnp.int32, factor.shape, 0)
    col_at = lax.broadcasted_iota(jnp.int32, factor.shape, 1)
    factor = jnp.where((col_at >= row_at) & (col_at < rank), factor, 0.0)
    factor = jnp.concatenate([factor, jnp.zeros((128 - rank, 128), jnp.float32)], axis=0)
    core_next_ref[...] = factor.T[:rank, :rank]


def truncate(gram_u, gram_v, core_matrix, sketch_seed, cells, samples):
    rank = core_matrix.shape[0]
    wide = gram_v.shape[0]
    block_core = jnp.kron(jnp.eye(wide // rank, dtype=jnp.float32), core_matrix)
    sketch_t = make_sketch(sketch_seed, wide, rank).T
    return pl.pallas_call(
        functools.partial(chain_kernel, rank, cells, samples),
        out_shape=(
            jax.ShapeDtypeStruct((rank, wide), jnp.float32),
            jax.ShapeDtypeStruct((rank, wide), jnp.float32),
            jax.ShapeDtypeStruct((rank, rank), jnp.float32),
        ),
        in_specs=[pl.BlockSpec(memory_space=pltpu.VMEM)] * 4,
        out_specs=(pl.BlockSpec(memory_space=pltpu.VMEM),) * 3,
        scratch_shapes=[pltpu.VMEM((wide, wide), jnp.float32), pltpu.VMEM((wide, wide), jnp.float32)],
        compiler_params=pltpu.CompilerParams(vmem_limit_bytes=24 * 1024 * 1024),
    )(gram_u, gram_v, block_core, sketch_t)


def local(
    u_factor,
    v_factor,
    mass_table,
    diffusivity_table,
    material_index,
    band_weights,
    band_offsets,
    core_matrix,
    sketch_seed,
):
    space_wide = widen_space(u_factor, mass_table, diffusivity_table, material_index)
    param_wide = widen_param(v_factor, band_weights, band_offsets)
    cells_total = u_factor.shape[1] * lax.axis_size("gx")
    samples_total = v_factor.shape[1] * lax.axis_size("pa")
    gram_u = lax.psum(gram_of(space_wide), "gx")
    gram_v = lax.psum(gram_of(param_wide), "pa")
    map_u_t, map_v_t, core_next = truncate(
        gram_u, gram_v, core_matrix, sketch_seed, cells_total, samples_total
    )
    u_next = matmul(map_u_t, space_wide)
    v_next = matmul(map_v_t, param_wide)
    return (u_next, v_next, core_next)


def solution(mesh):
    return jax.shard_map(
        local,
        mesh=mesh,
        in_specs=(
            P(None, "gx"),
            P(None, "pa"),
            P(),
            P(),
            P(None, "gx"),
            P(None, None, "pa"),
            P(),
            P(),
            P(),
        ),
        out_specs=(P(None, "gx"), P(None, "pa"), P()),
        check_vma=False,
    )
```

```python
import functools

import jax
import jax.numpy as jnp
from jax import lax
from jax.experimental import pallas as pl
from jax.experimental.pallas import tpu as pltpu
from jax.sharding import PartitionSpec as P

BAND = 4


MESH = pl.DeviceIdType.MESH
EDGE = 128


def push(src, dst, sems, at, axis, peer):
    return pltpu.make_async_remote_copy(
        src_ref=src,
        dst_ref=dst,
        send_sem=sems.at[0, at],
        recv_sem=sems.at[1, at],
        device_id={axis: peer},
        device_id_type=MESH,
    )


def edges_kernel(groups, parts, u_ref, v_ref, u_left, u_right, v_left, v_right, sems):
    barrier = pltpu.get_barrier_semaphore()
    rings = (("gx", groups), ("pa", parts))
    for axis, count in rings:
        me = lax.axis_index(axis)
        for step in (1, count - 1):
            pl.semaphore_signal(barrier, inc=1, device_id={axis: lax.rem(me + step, count)}, device_id_type=MESH)
    pl.semaphore_wait(barrier, 4)
    copies = []
    for at, ((axis, count), ref, left, right) in enumerate(
        zip(rings, (u_ref, v_ref), (u_left, v_left), (u_right, v_right))
    ):
        me = lax.axis_index(axis)
        length = ref.shape[1]
        copies.append(push(ref.at[:, length - EDGE :], left, sems, 2 * at, axis, lax.rem(me + 1, count)))
        copies.append(push(ref.at[:, :EDGE], right, sems, 2 * at + 1, axis, lax.rem(me + count - 1, count)))
    for copy in copies:
        copy.start()
    for copy in copies:
        copy.wait()


def edges(u_factor, v_factor):
    groups, parts = lax.axis_size("gx"), lax.axis_size("pa")
    rank = u_factor.shape[0]
    found = pl.pallas_call(
        functools.partial(edges_kernel, groups, parts),
        out_shape=(jax.ShapeDtypeStruct((rank, EDGE), jnp.float32),) * 4,
        in_specs=[pl.BlockSpec(memory_space=pl.ANY)] * 2,
        out_specs=(pl.BlockSpec(memory_space=pltpu.VMEM),) * 4,
        scratch_shapes=[pltpu.SemaphoreType.DMA((2, 4))],
        compiler_params=pltpu.CompilerParams(collective_id=0, has_side_effects=True),
    )(u_factor, v_factor)
    inner = (
        lax.axis_index("gx") > 0,
        lax.axis_index("gx") < groups - 1,
        lax.axis_index("pa") > 0,
        lax.axis_index("pa") < parts - 1,
    )
    return [jnp.where(keep, cells, 0.0) for keep, cells in zip(inner, found)]


def extended(cells, left, right, width):
    return jnp.concatenate([left[:, EDGE - width :], cells, right[:, :width]], axis=1)


def reduce_kernel(groups, parts, gu_ref, gv_ref, out_u, out_v, in_u, in_v, sum_u, sum_v, sems_a, sems_b, sems_c, sems_d, sems_e):
    me_g, me_p = lax.axis_index("gx"), lax.axis_index("pa")
    barrier = pltpu.get_barrier_semaphore()
    for axis, me, count in (("gx", me_g, groups), ("pa", me_p, parts)):
        for step in range(1, count):
            pl.semaphore_signal(barrier, inc=1, device_id={axis: lax.rem(me + step, count)}, device_id_type=MESH)
    pl.semaphore_wait(barrier, groups + parts - 2)

    def spread(axis, me, count, sems, source, target):
        copies = []
        for step in range(1, count):
            peer = lax.rem(me + step, count)
            copies.append(push(source(step, peer), target(step), sems, step, axis, peer))
            copies[-1].start()
        return copies

    first_v = spread("pa", me_p, parts, sems_a, lambda step, peer: gv_ref.at[peer], lambda step: in_v.at[step])
    first_u = spread("gx", me_g, groups, sems_b, lambda step, peer: gu_ref.at[peer], lambda step: in_u.at[step])
    total = gv_ref[me_p]
    for step in range(1, parts):
        first_v[step - 1].wait_recv()
        total = total + in_v[step]
    sum_v[me_g, me_p] = total
    second_v = spread("pa", me_p, parts, sems_c, lambda step, peer: sum_v.at[me_g, me_p], lambda step: sum_v.at[me_g, me_p])
    total = gu_ref[me_g]
    for step in range(1, groups):
        first_u[step - 1].wait_recv()
        total = total + in_u[step]
    sum_u[me_g] = total
    for copy in second_v:
        copy.wait_recv()
    third_v = spread("gx", me_g, groups, sems_d, lambda step, peer: sum_v.at[me_g], lambda step: sum_v.at[me_g])
    second_u = spread("gx", me_g, groups, sems_e, lambda step, peer: sum_u.at[me_g], lambda step: sum_u.at[me_g])
    for copy in third_v + second_u:
        copy.wait_recv()
    for copy in first_v + first_u + second_v + third_v + second_u:
        copy.wait_send()
    out_v[...] = sum_v[...]
    out_u[...] = sum_u[...]


def reduce_grams(gram_u, gram_v_rows):
    groups, parts = lax.axis_size("gx"), lax.axis_size("pa")
    wide = gram_u.shape[0]
    shape_u = (groups, wide // groups, wide)
    shape_v = (parts, wide // groups // parts, wide)
    every_v = (groups,) + shape_v
    vmem = pl.BlockSpec(memory_space=pltpu.VMEM)
    sum_u, sum_v = pl.pallas_call(
        functools.partial(reduce_kernel, groups, parts),
        out_shape=(jax.ShapeDtypeStruct(shape_u, jnp.float32), jax.ShapeDtypeStruct(every_v, jnp.float32)),
        in_specs=[vmem, vmem],
        out_specs=(vmem, vmem),
        scratch_shapes=[
            pltpu.VMEM(shape_u, jnp.float32),
            pltpu.VMEM(shape_v, jnp.float32),
            pltpu.VMEM(shape_u, jnp.float32),
            pltpu.VMEM(every_v, jnp.float32),
            pltpu.SemaphoreType.DMA((2, parts)),
            pltpu.SemaphoreType.DMA((2, groups)),
            pltpu.SemaphoreType.DMA((2, parts)),
            pltpu.SemaphoreType.DMA((2, groups)),
            pltpu.SemaphoreType.DMA((2, groups)),
        ],
        compiler_params=pltpu.CompilerParams(
            collective_id=1, has_side_effects=True, vmem_limit_bytes=24 * 1024 * 1024
        ),
    )(gram_u.reshape(shape_u), gram_v_rows.reshape(shape_v))
    return sum_u.reshape(wide, wide), sum_v.reshape(wide, wide)


def make_sketch(sketch_seed, wide, rank):
    rows_idx = lax.broadcasted_iota(jnp.int32, (wide, rank), 0)
    cols_idx = lax.broadcasted_iota(jnp.int32, (wide, rank), 1)
    first = (rows_idx * 131 + cols_idx * 977 + sketch_seed[0]) % 65521
    second = first * 7919 % 65521
    upper = second // 256
    lower = second % 256
    third = (upper * upper * 15 + 512 * upper * lower + lower * lower) % 65521
    fourth = (third * 30011 + rows_idx * 17 + cols_idx) % 65521
    return ((fourth.astype(jnp.float32) + 0.5) / 65521.0 - 0.5) * 3.4641


def matmul(left_m, right_m):
    return jnp.dot(
        left_m, right_m, precision=lax.Precision.HIGHEST, preferred_element_type=jnp.float32
    )


def solve_lower(lower_m, rhs, transpose):
    return lax.linalg.triangular_solve(
        lower_m, rhs, left_side=True, lower=True, transpose_a=transpose
    )


def widen_space(u_factor, left, right, mass_table, diffusivity_table, material_index):
    stencils = mass_table.shape[0]
    choices_m = jnp.arange(mass_table.shape[1], dtype=jnp.int32)
    onehot = (material_index[:, None, :] == choices_m[None, :, None]).astype(jnp.float32)
    mass_cell = jnp.sum(mass_table[:, :, None] * onehot, axis=1)
    diffusion = jnp.sum(diffusivity_table[:, :, None] * onehot, axis=1)
    padded = extended(u_factor, left, right, 1)
    laplace = padded[:, 2:] - 2.0 * u_factor + padded[:, :-2]
    blocks = mass_cell[:, None, :] * u_factor[None] + diffusion[:, None, :] * laplace[None]
    return blocks.reshape(stencils * u_factor.shape[0], u_factor.shape[1])


def widen_param(v_factor, left, right, band_weights, band_offsets):
    count = v_factor.shape[1]
    padded = extended(v_factor, left, right, BAND)
    blocks = []
    for stencil in range(band_weights.shape[0]):
        total = jnp.zeros(v_factor.shape, jnp.float32)
        for tap_index in range(band_weights.shape[1]):
            start = BAND + band_offsets[stencil, tap_index]
            moved = lax.dynamic_slice_in_dim(padded, start, count, 1)
            total = total + band_weights[stencil, tap_index][None, :] * moved
        blocks.append(total)
    return jnp.concatenate(blocks, axis=0)


def dot_nn(a, b):
    return lax.dot_general(a, b, (((1,), (0,)), ((), ())), precision=lax.Precision.HIGHEST, preferred_element_type=jnp.float32)


def dot_nt(a, b):
    return lax.dot_general(a, b, (((1,), (1,)), ((), ())), precision=lax.Precision.HIGHEST, preferred_element_type=jnp.float32)


def dot_tn(a, b):
    return lax.dot_general(a, b, (((0,), (0,)), ((), ())), precision=lax.Precision.HIGHEST, preferred_element_type=jnp.float32)


def eliminate(block, first):
    tile = 8
    count = block.shape[0] // tile
    lanes = 128
    wide = block.shape[1] // lanes
    rows = [block[tile * i : tile * (i + 1), :] for i in range(count)]
    sub = lax.broadcasted_iota(jnp.int32, (tile, lanes), 0)

    def spread(x):
        return jnp.concatenate([x] * wide, axis=1) if wide > 1 else x

    for q in range(count):
        at = first + tile * q
        cols = [
            {i: jnp.broadcast_to(rows[i][:, at + k : at + k + 1], (tile, lanes)) for i in range(q, count)}
            for k in range(tile)
        ]
        for j in range(tile):
            scale = lax.rsqrt(cols[j][q][j : j + 1, :])
            low = {i: cols[j][i] * scale for i in range(q, count)}
            for k in range(j + 1, tile):
                pivot = low[q][k : k + 1, :]
                for i in range(q, count):
                    cols[k][i] = cols[k][i] - low[i] * pivot
            own = rows[q][j : j + 1, :] * spread(scale)
            below = spread(jnp.where(sub > j, low[q], 0.0))
            rows[q] = jnp.where(spread(sub) == j, own, rows[q] - below * own)
            for i in range(q + 1, count):
                rows[i] = rows[i] - spread(low[i]) * own
    return jnp.concatenate(rows, axis=0)


def chain_kernel(rank, cells, samples, gram_u_ref, gram_v_ref, core_ref, sketch_ref, map_u_ref, map_v_ref, core_next_ref, gv, upper):
    wide = gram_u_ref.shape[0]
    gv[...] = gram_v_ref[...] * (1.0 / samples)
    for p in range(wide // rank):
        left = (p * rank) // 128 * 128
        low = p * rank
        part = gv[low : low + rank, left:]
        if p > 0:
            part = part - dot_tn(upper[:low, low : low + rank], upper[:low, left:])
        part = eliminate(part, low - left)
        row_at = lax.broadcasted_iota(jnp.int32, part.shape, 0) + low
        col_at = lax.broadcasted_iota(jnp.int32, part.shape, 1) + left
        upper[low : low + rank, left:] = jnp.where(col_at >= row_at, part, 0.0)
        if left > 0:
            upper[low : low + rank, :left] = jnp.zeros((rank, left), jnp.float32)
    core = core_ref[...]
    base = dot_nt(dot_nn(sketch_ref[...], upper[...]), core)
    seen = dot_nn(base, gram_u_ref[...] * (1.0 / cells))
    fill = jnp.zeros((128 - rank, wide), jnp.float32)
    square = dot_nt(base, jnp.concatenate([seen, fill], axis=0))
    back = dot_nn(seen, core)
    done = eliminate(jnp.concatenate([square, base, back], axis=1), 0)
    map_u_ref[...] = done[:, 128 : 128 + wide]
    back = done[:, 128 + wide :]
    square = dot_nt(dot_nn(back, gv[...]), jnp.concatenate([back, fill], axis=0))
    done = eliminate(jnp.concatenate([square, back], axis=1), 0)
    map_v_ref[...] = done[:, 128:]
    factor = done[:, :128]
    row_at = lax.broadcasted_iota(jnp.int32, factor.shape, 0)
    col_at = lax.broadcasted_iota(jnp.int32, factor.shape, 1)
    factor = jnp.where((col_at >= row_at) & (col_at < rank), factor, 0.0)
    factor = jnp.concatenate([factor, jnp.zeros((128 - rank, 128), jnp.float32)], axis=0)
    core_next_ref[...] = factor.T[:rank, :rank]


def truncate(gram_u, gram_v, core_matrix, sketch_seed, cells, samples):
    rank = core_matrix.shape[0]
    wide = gram_v.shape[0]
    block_core = jnp.kron(jnp.eye(wide // rank, dtype=jnp.float32), core_matrix)
    sketch_t = make_sketch(sketch_seed, wide, rank).T
    return pl.pallas_call(
        functools.partial(chain_kernel, rank, cells, samples),
        out_shape=(
            jax.ShapeDtypeStruct((rank, wide), jnp.float32),
            jax.ShapeDtypeStruct((rank, wide), jnp.float32),
            jax.ShapeDtypeStruct((rank, rank), jnp.float32),
        ),
        in_specs=[pl.BlockSpec(memory_space=pltpu.VMEM)] * 4,
        out_specs=(pl.BlockSpec(memory_space=pltpu.VMEM),) * 3,
        scratch_shapes=[pltpu.VMEM((wide, wide), jnp.float32), pltpu.VMEM((wide, wide), jnp.float32)],
        compiler_params=pltpu.CompilerParams(vmem_limit_bytes=24 * 1024 * 1024),
    )(gram_u, gram_v, block_core, sketch_t)


def local(
    u_factor,
    v_factor,
    mass_table,
    diffusivity_table,
    material_index,
    band_weights,
    band_offsets,
    core_matrix,
    sketch_seed,
):
    u_left, u_right, v_left, v_right = edges(u_factor, v_factor)
    space_wide = widen_space(u_factor, u_left, u_right, mass_table, diffusivity_table, material_index)
    param_wide = widen_param(v_factor, v_left, v_right, band_weights, band_offsets)
    groups = lax.axis_size("gx")
    cells_total = u_factor.shape[1] * groups
    samples_total = v_factor.shape[1] * lax.axis_size("pa")
    share = param_wide.shape[0] // groups
    own_rows = lax.dynamic_slice_in_dim(param_wide, lax.axis_index("gx") * share, share, 0)
    gram_u, gram_v = reduce_grams(dot_nt(space_wide, space_wide), dot_nt(own_rows, param_wide))
    map_u_t, map_v_t, core_next = truncate(
        gram_u, gram_v, core_matrix, sketch_seed, cells_total, samples_total
    )
    u_next = matmul(map_u_t, space_wide)
    v_next = matmul(map_v_t, param_wide)
    return (u_next, v_next, core_next)


def solution(mesh):
    return jax.shard_map(
        local,
        mesh=mesh,
        in_specs=(
            P(None, "gx"),
            P(None, "pa"),
            P(),
            P(),
            P(None, "gx"),
            P(None, None, "pa"),
            P(),
            P(),
            P(),
        ),
        out_specs=(P(None, "gx"), P(None, "pa"), P()),
        check_vma=False,
    )
```
